128 devices in a mesh: ctx: 16 (over y, x_hi, core), tp: 8 (over z, x_lo).
Axes of the slice: x: 4 (x_hi: 2, x_lo: 2; x = x_hi * 2 + x_lo), y: 4, z: 4, core: 2. Of those that a mesh axis runs over, the one named last changes fastest.
Arguments:
- text_states: bfloat16 [4096, 8192], P('ctx'), may hold values from -6 to 6
- image_states: bfloat16 [6144, 7680], P('ctx', 'tp'), may hold values from -6 to 6
- counts: int32 [16], replicated, may hold values from 336 to 384, as said below
- norm_gain: float32 [8192], replicated, may hold values from 0.5 to 1.5
- w_query: bfloat16 [8192, 4096], P(None, 'tp'), may hold values from -0.0625 to 0.0625
- q_gain: float32 [128], replicated
- w_key: bfloat16 [7680, 1024], P('tp'), may hold values from -0.09375 to 0.09375
- w_value: bfloat16 [7680, 1024], P('tp'), may hold values from -0.09375 to 0.09375
- k_gain: float32 [128], replicated
- w_out: bfloat16 [4096, 8192], P('tp'), may hold values from -0.125 to 0.125
- attn_gate: float32 [1], replicated, may hold values from 0.3 to 1.2
Outputs:
- layer_out: bfloat16 [4096, 8192], P('ctx', 'tp')
The draws below stay inside these ranges and needn't reach their ends.
Inputs may be any that keep to these rules, and one draw needn't show every extreme that they name: counts[c] live image slots stand first among the 384 slots of index c of ctx; the rest are padding. counts lie within 48 of 384, and some index has all 384 slots live.
All inputs are finite; a program needn't handle non-finite values.
Results may differ from the reference program's by a relative error of at most 0.0142.
The reference program's roundings to bfloat16 on the way count: a program that leaves them out, or rounds other values in their place, can miss the bound.
Values may be sent and summed in bfloat16 or wider, within the bound.
No kernel may reach another device: no remote copies, remote signals or barrier semaphores. Data moves between devices by JAX's collectives and lax.ppermute only.
A program may use at most 128 MiB of HBM per device.

```python
import jax
import jax.numpy as jnp
from jax import lax

D = 8192
QH = 32
KVH = 8
HD = 128
VD = 7680
IMG_CAP = 384
TOKENS = 4096
IMG_SLOTS = 6144
N_CTX = 16
N_TP = 8


def draw_q_gain(key, part):
    key = jax.random.fold_in(key, 11)
    return jax.random.uniform(key, (HD,), jnp.float32, 1.2, 2.6)


def draw_k_gain(key, part):
    key = jax.random.fold_in(key, 23)
    return jax.random.uniform(key, (HD,), jnp.float32, 1.2, 2.6)


def draw_counts(key, part):
    key = jax.random.fold_in(key, 5)
    shortfall = jax.random.randint(jax.random.fold_in(key, 1), (N_CTX,), 0, IMG_CAP // 8 + 1)
    full_rank = jax.random.randint(jax.random.fold_in(key, 2), (), 0, N_CTX)
    rank_ids = jnp.arange(N_CTX, dtype=jnp.int32)
    return jnp.where(rank_ids == full_rank, IMG_CAP, IMG_CAP - shortfall).astype(jnp.int32)


def with_spikes(result, own_key, source, target, parts, factor):
    def block_of(axis_at):
        return (jnp.arange(result.shape[axis_at]) // (result.shape[axis_at] // parts)).reshape((-1,) + (1,) * (result.ndim - 1 - axis_at))

    near = jax.random.permutation(own_key, parts)[block_of(target)]
    second = (block_of(target) + parts // 2) % parts
    return jnp.where((block_of(source) == near) | (block_of(source) == second), factor * result, result)


def level_of(stream_key, shape, split, smallest, largest):
    def one(axis_at, parts):
        heights = jax.random.uniform(jax.random.fold_in(jax.random.fold_in(stream_key, 6), axis_at), (parts,), jnp.float32, smallest / len(split), largest / len(split))
        return jnp.repeat(jnp.exp(heights), shape[axis_at] // parts).reshape((-1,) + (1,) * (len(shape) - axis_at - 1))

    factor_of = one(*split[0])
    for cut in split[1:]:
        factor_of = factor_of * one(*cut)
    return factor_of


def centred(rng, dims, width, reach, shards=(), kind=jnp.bfloat16):
    loudness = level_of(rng, dims, shards, -0.22, 0.18) if shards else 1.0
    result = jax.random.normal(rng, dims, jnp.float32) * width * loudness
    return jnp.minimum(jnp.maximum(result, -reach), reach).astype(kind)


def heavy_noise(rng, shape, spread, limit, pieces, heavy, held_as=jnp.bfloat16):
    drawn = spread * jax.random.normal(rng, shape, jnp.float32)
    if pieces:
        drawn = drawn * level_of(rng, shape, pieces, -0.22, 0.18)
    return jnp.clip(with_spikes(drawn, jax.random.fold_in(rng, 3), *heavy), -limit, limit).astype(held_as)


def setup_inputs(seed: int = 0) -> dict:
    keys = jax.random.split(jax.random.key(seed), 12)
    text_states = centred(keys[0], (TOKENS, D), 1.0, 6.0, ((0, 16),))
    image_states = centred(keys[1], (IMG_SLOTS, VD), 1.0, 6.0, ((0, 16), (1, 8)))
    counts = draw_counts(jax.random.fold_in(keys[11], 71), 0)
    norm_gain = jnp.clip(1.0 + 0.1 * jax.random.normal(keys[3], (D,), jnp.float32), 0.5, 1.5)
    w_query = centred(keys[4], (D, QH * HD), D ** -0.5, 0.0625, ((1, 8),))
    q_gain = draw_q_gain(jax.random.fold_in(keys[11], 71), 0)
    w_key = heavy_noise(keys[6], (VD, KVH * HD), VD ** -0.5, 0.09375, ((0, 8),), (0, 1, 8, 2.0))
    w_value = heavy_noise(keys[7], (VD, KVH * HD), VD ** -0.5, 0.09375, ((0, 8),), (0, 1, 8, 2.0))
    k_gain = draw_k_gain(jax.random.fold_in(keys[11], 71), 0)
    w_out = heavy_noise(keys[9], (QH * HD, D), (QH * HD) ** -0.5, 0.125, ((0, 8),), (0, 1, 8, 2.0))
    attn_gate = jnp.clip(jax.random.uniform(keys[10], (1,), jnp.float32, 0.3, 1.2), 0.3, 1.2)
    return {"text_states": text_states, "image_states": image_states, "counts": counts, "norm_gain": norm_gain, "w_query": w_query, "q_gain": q_gain, "w_key": w_key, "w_value": w_value, "k_gain": k_gain, "w_out": w_out, "attn_gate": attn_gate}


epsilon = 1e-05

def rms_scale(values, scale_gain):
    mean_square = lax.optimization_barrier(jnp.mean(values * values, axis=-1, keepdims=True))
    return values * lax.rsqrt(mean_square + epsilon) * scale_gain

def reference(text_states, image_states, counts, norm_gain, w_query, q_gain, w_key, w_value, k_gain, w_out, attn_gate):
    text_wide = text_states.astype(jnp.float32)
    normed = rms_scale(text_wide, norm_gain).astype(jnp.bfloat16)
    group_size = QH // KVH
    query_rows = jnp.dot(normed, w_query, preferred_element_type=jnp.float32).reshape(TOKENS, KVH, group_size, HD)
    query_rows = rms_scale(query_rows, q_gain).astype(jnp.bfloat16)
    key_rows = jnp.dot(image_states, w_key, preferred_element_type=jnp.float32).reshape(IMG_SLOTS, KVH, HD)
    key_rows = rms_scale(key_rows, k_gain).astype(jnp.bfloat16)
    value_rows = jnp.dot(image_states, w_value, preferred_element_type=jnp.float32).astype(jnp.bfloat16)
    value_rows = value_rows.reshape(IMG_SLOTS, KVH, HD)
    slot_ids = jnp.arange(IMG_SLOTS, dtype=jnp.int32)
    owner_rank = slot_ids // IMG_CAP
    slot_limit = counts[owner_rank]
    is_live = slot_ids - owner_rank * IMG_CAP < slot_limit
    score_scale = HD ** (-0.5)

    def one_head(operands):
        head_query, head_keys, head_values = operands
        flat_query = head_query.reshape(TOKENS * group_size, HD)
        score = jnp.dot(flat_query, head_keys.T, preferred_element_type=jnp.float32) * score_scale
        score = jnp.where(is_live[None, :], score, -jnp.inf)
        row_top = lax.optimization_barrier(jnp.max(score, axis=1, keepdims=True))
        exp_terms = jnp.exp(score - row_top)
        row_total = lax.optimization_barrier(jnp.sum(exp_terms, axis=1, keepdims=True))
        weighted = jnp.dot(exp_terms.astype(jnp.bfloat16), head_values, preferred_element_type=jnp.float32)
        return (weighted / row_total).astype(jnp.bfloat16).reshape(TOKENS, group_size, HD)
    attended = lax.map(one_head, (query_rows.transpose(1, 0, 2, 3), key_rows.transpose(1, 0, 2), value_rows.transpose(1, 0, 2)))
    attended = attended.transpose(1, 0, 2, 3).reshape(TOKENS, QH * HD)
    slice_width = QH * HD // N_TP
    projected = jnp.zeros((TOKENS, D), jnp.float32)
    for rank_id in range(N_TP):
        head_part = jnp.dot(attended[:, rank_id * slice_width:(rank_id + 1) * slice_width], w_out[rank_id * slice_width:(rank_id + 1) * slice_width, :], preferred_element_type=jnp.float32)
        rounded = lax.optimization_barrier(head_part.astype(jnp.bfloat16))
        projected = projected + rounded.astype(jnp.float32)
    return (text_wide + jnp.tanh(attn_gate[0]) * projected).astype(jnp.bfloat16)
```

```python
import functools
import math

import jax
import jax.numpy as jnp
from jax import lax
from jax.experimental import pallas as pl
from jax.experimental.pallas import tpu as pltpu
from jax.sharding import PartitionSpec as P

epsilon = 1e-05
HEAD = 128
TP_SHIFTS = [(2, 1), (2, 0), (1, 1), (3, 1), (1, 0), (3, 0), (0, 1)]
RING = [2, 1, 3]
SMEM = pl.BlockSpec(memory_space=pltpu.SMEM)
VMEM = pl.BlockSpec(memory_space=pltpu.VMEM)
HBM = pl.BlockSpec(memory_space=pltpu.HBM)
HINT = pl.CostEstimate(flops=1 << 20, bytes_accessed=1 << 10, transcendentals=0)


def tp_dest(index, shift):
    return (((index >> 1) + shift[0]) & 3) * 2 + ((index + shift[1]) & 1)


def ctx_dest(index, shift):
    y, xh, core = index >> 2, index >> 1, index
    return ((y + shift[0]) & 3) * 4 + ((xh + shift[1]) & 1) * 2 + ((core + shift[2]) & 1)


def tp_send(block, shift):
    return lax.ppermute(block, "tp", [(i, tp_dest(i, shift)) for i in range(8)])


def ctx_send(block, shift):
    return lax.ppermute(block, "ctx", [(i, ctx_dest(i, shift)) for i in range(16)])


def params(mib=48):
    return pltpu.CompilerParams(vmem_limit_bytes=mib * 1024 * 1024)


def rms_scale(values, scale_gain):
    mean_square = jnp.mean(values * values, axis=-1, keepdims=True)
    return values * lax.rsqrt(mean_square + epsilon) * scale_gain


def kv_kernel(image_ref, key_ref, value_ref, out_ref):
    image = image_ref[...].T
    for head in range(out_ref.shape[0]):
        lanes = slice(head * HEAD, (head + 1) * HEAD)
        weight = jnp.concatenate([key_ref[:, lanes], value_ref[:, lanes]], axis=1)
        out_ref[head] = jnp.dot(image, weight, preferred_element_type=jnp.float32).astype(jnp.bfloat16)


def project_kv(image, w_key, w_value):
    return pl.pallas_call(
        kv_kernel,
        out_shape=jax.ShapeDtypeStruct((w_key.shape[1] // HEAD, image.shape[1], 2 * HEAD), jnp.bfloat16),
        in_specs=[VMEM] * 3,
        out_specs=VMEM,
        compiler_params=params(),
        cost_estimate=HINT,
        name="project_kv",
    )(image, w_key, w_value)


def query_kernel(text_ref, gain_ref, weight_ref, head_gain_ref, out_ref, scale_ref, total_ref):
    step = pl.program_id(0)
    depth = weight_ref.shape[0]
    tiles = text_ref.shape[1] // depth

    @pl.when(step == 0)
    def _():
        square = None
        for at in range(0, text_ref.shape[1], HEAD):
            wide = text_ref[:, at : at + HEAD].astype(jnp.float32)
            square = wide * wide if square is None else square + wide * wide
        mean_square = jnp.sum(square, axis=1, keepdims=True) / text_ref.shape[1]
        scale_ref[...] = jnp.broadcast_to(lax.rsqrt(mean_square + epsilon), scale_ref.shape)

    columns = pl.ds(pl.multiple_of(step * depth, depth), depth)
    wide = text_ref[:, columns].astype(jnp.float32)
    normed = (wide * scale_ref[:, :1] * gain_ref[:, columns]).astype(jnp.bfloat16)
    product = jnp.dot(normed, weight_ref[...], preferred_element_type=jnp.float32)
    total_ref[...] = jnp.where(step == 0, product, total_ref[...] + product)

    @pl.when(step == tiles - 1)
    def _():
        for at in range(0, out_ref.shape[1], HEAD):
            head = total_ref[:, at : at + HEAD]
            out_ref[:, at : at + HEAD] = rms_scale(head, head_gain_ref[...]).astype(jnp.bfloat16)


def project_query(text, norm_gain, w_query, q_gain):
    rows, depth = text.shape
    width, tile = w_query.shape[1], depth // 8
    return pl.pallas_call(
        query_kernel,
        out_shape=jax.ShapeDtypeStruct((rows, width), jnp.bfloat16),
        grid=(depth // tile,),
        in_specs=[
            pl.BlockSpec((rows, depth), lambda step: (0, 0)),
            pl.BlockSpec((1, depth), lambda step: (0, 0)),
            pl.BlockSpec((tile, width), lambda step: (step, 0)),
            pl.BlockSpec((1, HEAD), lambda step: (0, 0)),
        ],
        out_specs=pl.BlockSpec((rows, width), lambda step: (0, 0)),
        scratch_shapes=[pltpu.VMEM((rows, HEAD), jnp.float32), pltpu.VMEM((rows, width), jnp.float32)],
        compiler_params=params(56),
        cost_estimate=HINT,
        name="project_query",
    )(text, norm_gain.reshape(1, depth), w_query, q_gain.reshape(1, HEAD))


def combine_kernel(gain_ref, parts_ref, out_ref):
    total = parts_ref[0].astype(jnp.float32)
    for at in range(1, parts_ref.shape[0]):
        total = total + parts_ref[at].astype(jnp.float32)
    out_ref[:, :HEAD] = rms_scale(total[:, :HEAD], gain_ref[...]).astype(jnp.bfloat16)
    out_ref[:, HEAD:] = total[:, HEAD:].astype(jnp.bfloat16)


def combine_kv(gain, parts):
    return pl.pallas_call(
        combine_kernel,
        out_shape=jax.ShapeDtypeStruct(parts.shape[1:], jnp.bfloat16),
        in_specs=[VMEM] * 2,
        out_specs=VMEM,
        compiler_params=params(),
        cost_estimate=HINT,
        name="combine_kv",
    )(gain.reshape(1, HEAD), parts)


def attend_kernel(shifts, first, last, me_ref, counts_ref, query_ref, *refs):
    stacks, refs = refs[: len(shifts)], refs[len(shifts) :]
    if not first:
        held_in, refs = refs[:3], refs[3:]
    heads = query_ref.shape[1] // HEAD
    capacity = stacks[0].shape[0] // 2
    factor = HEAD ** (-0.5) * math.log2(math.e)
    slot = lax.broadcasted_iota(jnp.int32, (1, HEAD), 1) + (capacity - HEAD)
    for head in range(heads):
        lanes = slice(head * HEAD, (head + 1) * HEAD)
        query = query_ref[:, lanes]
        if not first:
            acc = held_in[0][:, lanes]
            top = held_in[1][:, head : head + 1]
            total = held_in[2][:, head : head + 1]
        for at, ((ring, core), stack) in enumerate(zip(shifts, stacks)):
            score = lax.dot_general(
                query, stack[:, :HEAD], (((1,), (1,)), ((), ())), preferred_element_type=jnp.float32
            )
            pieces = []
            for half in range(2):
                live = slot < counts_ref[ctx_dest(me_ref[0], (-ring, half, core))]
                start, stop = half * capacity, (half + 1) * capacity
                pieces.append(score[:, start : stop - HEAD])
                pieces.append(jnp.where(live, score[:, stop - HEAD : stop], -jnp.inf))
            score = jnp.concatenate(pieces, axis=1)
            block_top = jnp.max(score, axis=1, keepdims=True) * factor
            fresh = first and at == 0
            new_top = block_top if fresh else jnp.maximum(top, block_top)
            weights = jnp.exp2(score * factor - new_top)
            block_total = jnp.sum(weights, axis=1, keepdims=True)
            block_acc = jnp.dot(weights.astype(jnp.bfloat16), stack[:, HEAD:], preferred_element_type=jnp.float32)
            if fresh:
                total, acc = block_total, block_acc
            else:
                decay = jnp.exp2(top - new_top)
                total, acc = total * decay + block_total, acc * decay + block_acc
            top = new_top
        if last:
            refs[0][:, lanes] = (acc / total).astype(jnp.bfloat16)
        else:
            refs[0][:, lanes] = acc
            refs[1][:, head : head + 1] = top
            refs[2][:, head : head + 1] = total


def attend(me, counts, query, blocks, shifts, held, last):
    rows, width = query.shape
    if last:
        out_shape = [jax.ShapeDtypeStruct((rows, width), jnp.bfloat16)]
    else:
        out_shape = [jax.ShapeDtypeStruct((rows, width), jnp.float32)]
        out_shape += [jax.ShapeDtypeStruct((rows, HEAD), jnp.float32)] * 2
    held = list(held or [])
    return pl.pallas_call(
        functools.partial(attend_kernel, shifts, not held, last),
        out_shape=out_shape,
        in_specs=[SMEM, SMEM] + [VMEM] * (1 + len(blocks) + len(held)),
        out_specs=[VMEM] * len(out_shape),
        compiler_params=params(),
        cost_estimate=HINT,
        name="attend",
    )(me, counts, query, *blocks, *held)


def cut_weights(ctx_me, tp_me, w_out):
    rows, tile = w_out.shape[0] // 4, w_out.shape[1] // 16
    y, core, xl = ctx_me >> 2, ctx_me & 1, (tp_me + 1) & 1
    slab = lax.dynamic_slice_in_dim(w_out, y * rows, rows, 0, allow_negative_indices=False)
    first = xl * 2 + core
    return jnp.concatenate(
        [
            lax.dynamic_slice_in_dim(slab, (z * 4 + first) * tile, tile, 1, allow_negative_indices=False)
            for z in range(4)
        ],
        axis=1,
    )


def own_kernel(me_ref, gate_ref, attended_ref, weight_ref, text_ref, *refs):
    outs, (weights, text, sems) = refs[:4], refs[4:]
    width = text.shape[1]
    copies = []
    for at, ring in enumerate(RING + [0]):
        column = pl.multiple_of(tp_dest(me_ref[1], (ring, 0)) * width, width)
        copies.append(pltpu.make_async_copy(weight_ref.at[:, pl.ds(column, width)], weights.at[at], sems.at[at]))
    column = pl.multiple_of(me_ref[1] * width, width)
    copies.append(pltpu.make_async_copy(text_ref.at[:, pl.ds(column, width)], text, sems.at[4]))
    for copy in copies:
        copy.start()
    for at, out in enumerate(outs):
        copies[at].wait()
        total = jnp.dot(attended_ref[...], weights[at], preferred_element_type=jnp.float32)
        if at == 3:
            copies[4].wait()
            total = text[...].astype(jnp.float32) + gate_ref[...] * total
        out[...] = total


def project_own(me, gate, attended, w_out, text):
    rows, width = attended.shape[0], w_out.shape[1] // 8
    return pl.pallas_call(
        own_kernel,
        out_shape=[jax.ShapeDtypeStruct((rows, width), jnp.float32)] * 4,
        in_specs=[SMEM, VMEM, VMEM, HBM, HBM],
        out_specs=[VMEM] * 4,
        scratch_shapes=[
            pltpu.VMEM((4, w_out.shape[0], width), jnp.bfloat16),
            pltpu.VMEM((rows, width), jnp.bfloat16),
            pltpu.SemaphoreType.DMA((5,)),
        ],
        compiler_params=params(32),
        cost_estimate=HINT,
        name="project_own",
    )(me, gate, attended, w_out, text)


def out_kernel(ring, me_ref, gate_ref, swapped_ref, own_ref, *refs):
    mine, other, out = refs[:4], refs[4:8], refs[8]
    y, core, z = me_ref[0] >> 2, me_ref[0] & 1, me_ref[1] >> 1
    rows = mine[0].shape[0]
    tile = mine[0].shape[1] // 4
    swapped = jnp.concatenate(
        [swapped_ref[:, pl.ds(pl.multiple_of(((y - back) & 3) * rows, rows), rows)] for back in [0] + RING], axis=1
    )
    source = pl.ds(pl.multiple_of(((z + ring) & 3) * tile, tile), tile)
    for half, pieces in ((core, mine), (1 - core, other)):
        target = pl.ds(pl.multiple_of(half * tile, tile), tile)
        weight = jnp.concatenate([piece[:, source] for piece in pieces], axis=0)
        product = jnp.dot(swapped, weight, preferred_element_type=jnp.float32)
        if ring == 0:
            product = gate_ref[...] * product
        out[:, target] = (own_ref[:, target] + product).astype(out.dtype)


def project_out(ring, me, gate, swapped, own, mine, other):
    return pl.pallas_call(
        functools.partial(out_kernel, ring),
        out_shape=jax.ShapeDtypeStruct(own.shape, jnp.bfloat16 if ring else jnp.float32),
        in_specs=[SMEM] + [VMEM] * (3 + len(mine) + len(other)),
        out_specs=VMEM,
        compiler_params=params(32),
        cost_estimate=HINT,
        name="project_out",
    )(me, gate, swapped, own, *mine, *other)


def add_kernel(base_ref, gate_ref, *refs):
    total = refs[0][...].astype(jnp.float32)
    for ref in refs[1:-1]:
        total = total + ref[...].astype(jnp.float32)
    refs[-1][...] = (base_ref[...] + gate_ref[...] * total).astype(jnp.bfloat16)


def local(
    text_states,
    image_states,
    counts,
    norm_gain,
    w_query,
    q_gain,
    w_key,
    w_value,
    k_gain,
    w_out,
    attn_gate,
):
    tp_me = lax.axis_index("tp")
    ctx_me = lax.axis_index("ctx")
    ctx_row = ctx_me.astype(jnp.int32).reshape(1)
    me = jnp.stack([ctx_me, tp_me]).astype(jnp.int32)

    cut = cut_weights(ctx_me, tp_me, w_out)
    image_states, text_first, cut = lax.optimization_barrier((image_states, text_states, cut))
    piece = tp_send(cut, (0, 1))
    sent = project_kv(image_states.T, w_key, w_value)
    query = project_query(text_first, norm_gain, w_query, q_gain)
    sent, piece, query = lax.optimization_barrier((sent, piece, query))
    mine = [piece] + [ctx_send(piece, (ring, 0, 0)) for ring in RING]
    arrived = lax.all_to_all(sent, "tp", 0, 0, tiled=True)
    own_kv = combine_kv(k_gain, arrived)

    across = ctx_send(own_kv, (0, 1, 0))
    stack = jnp.concatenate([own_kv, across], axis=0)
    stack, *mine = lax.optimization_barrier((stack, *mine))
    other = [ctx_send(block, (0, 0, 1)) for block in mine]
    far = [ctx_send(stack, (ring, 0, 0)) for ring in RING]
    near = ctx_send(stack, (0, 0, 1))
    held = attend(ctx_row, counts, query, [stack, near], [(0, 0), (0, 1)], None, False)
    *far, held_acc = lax.optimization_barrier((*far, held[0]))
    held = [held_acc, *held[1:]]
    near = [ctx_send(block, (0, 0, 1)) for block in far]
    held = attend(ctx_row, counts, query, far, [(ring, 0) for ring in RING], held, False)
    (attended,) = attend(ctx_row, counts, query, near, [(ring, 1) for ring in RING], held, True)

    gate = jnp.tanh(attn_gate).reshape(1, 1)
    swapped = tp_send(attended, (0, 1))
    own = project_own(me, gate, attended, w_out, text_states)
    arrived = []
    for ring, block in zip(RING, own):
        arrived.append(tp_send(project_out(ring, me, gate, swapped, block, mine, other), (ring, 0)))
    base = project_out(0, me, gate, swapped, own[3], mine, other)
    return pl.pallas_call(
        add_kernel,
        out_shape=jax.ShapeDtypeStruct(base.shape, jnp.bfloat16),
        in_specs=[VMEM] * (2 + len(arrived)),
        out_specs=VMEM,
        compiler_params=params(16),
        cost_estimate=HINT,
        name="add_residual",
    )(base, gate, *arrived)


def solution(mesh):
    in_specs = (
        P("ctx", None),
        P("ctx", "tp"),
        P(),
        P(),
        P(None, "tp"),
        P(),
        P("tp", None),
        P("tp", None),
        P(),
        P("tp", None),
        P(),
    )
    out_specs = P("ctx", "tp")
    return jax.shard_map(local, mesh=mesh, in_specs=in_specs, out_specs=out_specs, check_vma=False)
```

```python
import functools
import math

import jax
import jax.numpy as jnp
from jax import lax
from jax.experimental import pallas as pl
from jax.experimental.pallas import tpu as pltpu
from jax.sharding import PartitionSpec as P

epsilon = 1e-05
HEAD = 128
TP_SHIFTS = [(2, 1), (2, 0), (1, 1), (3, 1), (1, 0), (3, 0), (0, 1)]
RING = [2, 1, 3]
HOPS = [1, 2, 3, 0]
AROUND = [(2, 1), (0, 1), (1, 0), (3, 0), (2, 0), (1, 1), (3, 1), (0, 0)]
SMEM = pl.BlockSpec(memory_space=pltpu.SMEM)
VMEM = pl.BlockSpec(memory_space=pltpu.VMEM)
HBM = pl.BlockSpec(memory_space=pltpu.HBM)
HINT = pl.CostEstimate(flops=1 << 20, bytes_accessed=1 << 10, transcendentals=0)


def tp_dest(index, shift):
    return (((index >> 1) + shift[0]) & 3) * 2 + ((index + shift[1]) & 1)


def ctx_dest(index, shift):
    y, xh, core = index >> 2, index >> 1, index
    return ((y + shift[0]) & 3) * 4 + ((xh + shift[1]) & 1) * 2 + ((core + shift[2]) & 1)


def tp_send(block, shift):
    return lax.ppermute(block, "tp", [(i, tp_dest(i, shift)) for i in range(8)])


def hop_send(block, hop):
    return lax.ppermute(block, "tp", [(i, i ^ (2 * hop)) for i in range(8)])


def ctx_send(block, shift):
    return lax.ppermute(block, "ctx", [(i, ctx_dest(i, shift)) for i in range(16)])


def params(mib=48):
    return pltpu.CompilerParams(vmem_limit_bytes=mib * 1024 * 1024)


def rms_scale(values, scale_gain):
    mean_square = jnp.mean(values * values, axis=-1, keepdims=True)
    return values * lax.rsqrt(mean_square + epsilon) * scale_gain


def kv_kernel(image_ref, key_ref, value_ref, out_ref):
    image = image_ref[...].T
    for head in range(out_ref.shape[0]):
        lanes = slice(head * HEAD, (head + 1) * HEAD)
        weight = jnp.concatenate([key_ref[:, lanes], value_ref[:, lanes]], axis=1)
        out_ref[head] = jnp.dot(image, weight, preferred_element_type=jnp.float32).astype(jnp.bfloat16)


def project_kv(image, w_key, w_value):
    return pl.pallas_call(
        kv_kernel,
        out_shape=jax.ShapeDtypeStruct((w_key.shape[1] // HEAD, image.shape[1], 2 * HEAD), jnp.bfloat16),
        in_specs=[VMEM] * 3,
        out_specs=VMEM,
        compiler_params=params(),
        cost_estimate=HINT,
        name="project_kv",
    )(image, w_key, w_value)


def query_kernel(text_ref, gain_ref, weight_ref, head_gain_ref, out_ref, scale_ref, total_ref):
    step = pl.program_id(0)
    depth = weight_ref.shape[0]
    tiles = text_ref.shape[1] // depth

    @pl.when(step == 0)
    def _():
        square = None
        for at in range(0, text_ref.shape[1], HEAD):
            wide = text_ref[:, at : at + HEAD].astype(jnp.float32)
            square = wide * wide if square is None else square + wide * wide
        mean_square = jnp.sum(square, axis=1, keepdims=True) / text_ref.shape[1]
        scale_ref[...] = jnp.broadcast_to(lax.rsqrt(mean_square + epsilon), scale_ref.shape)

    columns = pl.ds(pl.multiple_of(step * depth, depth), depth)
    wide = text_ref[:, columns].astype(jnp.float32)
    normed = (wide * scale_ref[:, :1] * gain_ref[:, columns]).astype(jnp.bfloat16)
    product = jnp.dot(normed, weight_ref[...], preferred_element_type=jnp.float32)
    total_ref[...] = jnp.where(step == 0, product, total_ref[...] + product)

    @pl.when(step == tiles - 1)
    def _():
        rows = total_ref.shape[0]
        for at in range(total_ref.shape[1] // HEAD):
            head = total_ref[:, at * HEAD : (at + 1) * HEAD]
            out_ref[at * rows : (at + 1) * rows] = rms_scale(head, head_gain_ref[...]).astype(jnp.bfloat16)


def project_query(text, norm_gain, w_query, q_gain):
    rows, depth = text.shape
    width, tile = w_query.shape[1], depth // 8
    return pl.pallas_call(
        query_kernel,
        out_shape=jax.ShapeDtypeStruct((rows * width // HEAD, HEAD), jnp.bfloat16),
        grid=(depth // tile,),
        in_specs=[
            pl.BlockSpec((rows, depth), lambda step: (0, 0)),
            pl.BlockSpec((1, depth), lambda step: (0, 0)),
            pl.BlockSpec((tile, width), lambda step: (step, 0)),
            pl.BlockSpec((1, HEAD), lambda step: (0, 0)),
        ],
        out_specs=pl.BlockSpec((rows * width // HEAD, HEAD), lambda step: (0, 0)),
        scratch_shapes=[pltpu.VMEM((rows, HEAD), jnp.float32), pltpu.VMEM((rows, width), jnp.float32)],
        compiler_params=params(32),
        cost_estimate=HINT,
        name="project_query",
    )(text, norm_gain.reshape(1, depth), w_query, q_gain.reshape(1, HEAD))


def combine_kernel(gain_ref, parts_ref, out_ref):
    total = parts_ref[0].astype(jnp.float32)
    for at in range(1, parts_ref.shape[0]):
        total = total + parts_ref[at].astype(jnp.float32)
    keys = rms_scale(total[:, :HEAD], gain_ref[...]).astype(jnp.bfloat16)
    values = total[:, HEAD:].astype(jnp.bfloat16)
    out_ref[:, :HEAD] = keys
    out_ref[:, HEAD:] = values


def combine_kv(gain, parts):
    return pl.pallas_call(
        combine_kernel,
        out_shape=jax.ShapeDtypeStruct(parts.shape[1:], jnp.bfloat16),
        in_specs=[VMEM] * 2,
        out_specs=VMEM,
        compiler_params=params(),
        cost_estimate=HINT,
        name="combine_kv",
    )(gain.reshape(1, HEAD), parts)


def attend_kernel(flip, last, me_ref, counts_ref, query_ref, *refs):
    first = not last
    blocks, refs = refs[: len(AROUND)], refs[len(AROUND) :]
    if not first:
        held_in, refs = refs[:2], refs[2:]
    outs, (score_ref,) = refs[:-1], refs[-1:]
    capacity = blocks[0].shape[0]
    slots = len(blocks) * capacity
    factor = HEAD ** (-0.5) * math.log2(math.e)
    slot = lax.broadcasted_iota(jnp.int32, (1, HEAD), 1) + (capacity - HEAD)
    keys = jnp.concatenate([block[:, :HEAD] for block in blocks], axis=0)
    values = jnp.concatenate([block[:, HEAD:] for block in blocks], axis=0)
    values = jnp.concatenate([values, jnp.ones_like(values)], axis=1)
    score_ref[...] = lax.dot_general(
        query_ref[...], keys, (((1,), (1,)), ((), ())), preferred_element_type=jnp.float32
    )
    live = [slot < counts_ref[ctx_dest(me_ref[0], (-y, -xh, flip))] for y, xh in AROUND]
    rows = 256
    for start in range(0, query_ref.shape[0], rows):
        band = slice(start, start + rows)
        pieces = []
        for at in range(0, slots, HEAD):
            piece = score_ref[band, at : at + HEAD]
            if at % capacity == capacity - HEAD:
                piece = jnp.where(live[at // capacity], piece, -jnp.inf)
            pieces.append(piece)
        top = functools.reduce(jnp.maximum, pieces)
        top = jnp.max(top, axis=1, keepdims=True) * factor
        if not first:
            top = jnp.maximum(held_in[1][band, :1], top)
        weights = [jnp.exp2(piece * factor - top).astype(jnp.bfloat16) for piece in pieces]
        acc = jnp.dot(jnp.concatenate(weights, axis=1), values, preferred_element_type=jnp.float32)
        if not first:
            acc = acc + held_in[0][band] * jnp.exp2(held_in[1][band, :1] - top)
        if last:
            lanes = slice(start // rows * HEAD, (start // rows + 1) * HEAD)
            outs[0][:, lanes] = (acc[:, :HEAD] / acc[:, HEAD:]).astype(jnp.bfloat16)
        else:
            outs[0][band] = acc
            outs[1][band] = jnp.broadcast_to(top, (rows, HEAD))


def attend(me, counts, query, blocks, flip, held=()):
    rows = query.shape[0]
    if held:
        out_shape = [jax.ShapeDtypeStruct((256, rows * HEAD // 256), jnp.bfloat16)]
    else:
        out_shape = [jax.ShapeDtypeStruct((rows, width), jnp.float32) for width in (2 * HEAD, HEAD)]
    return pl.pallas_call(
        functools.partial(attend_kernel, flip, bool(held)),
        out_shape=out_shape,
        in_specs=[SMEM, SMEM] + [VMEM] * (1 + len(blocks) + len(held)),
        out_specs=[VMEM] * len(out_shape),
        scratch_shapes=[pltpu.VMEM((rows, len(blocks) * blocks[0].shape[0]), jnp.float32)],
        compiler_params=params(),
        cost_estimate=HINT,
        name="attend",
    )(me, counts, query, *blocks, *held)


def cut_weights(ctx_me, tp_me, w_out):
    rows, tile = w_out.shape[0] // 4, w_out.shape[1] // 16
    y, core, xl = ctx_me >> 2, ctx_me & 1, (tp_me + 1) & 1
    slab = lax.dynamic_slice_in_dim(w_out, y * rows, rows, 0, allow_negative_indices=False)
    first = xl * 2 + core
    return jnp.concatenate(
        [
            lax.dynamic_slice_in_dim(slab, (z * 4 + first) * tile, tile, 1, allow_negative_indices=False)
            for z in range(4)
        ],
        axis=1,
    )


def own_kernel(me_ref, gate_ref, attended_ref, weight_ref, text_ref, *refs):
    outs, (weights, text, sems) = refs[:4], refs[4:]
    width = text.shape[1]
    copies = []
    for at, hop in enumerate(HOPS):
        column = pl.multiple_of((me_ref[1] ^ (2 * hop)) * width, width)
        copies.append(pltpu.make_async_copy(weight_ref.at[:, pl.ds(column, width)], weights.at[at], sems.at[at]))
    column = pl.multiple_of(me_ref[1] * width, width)
    copies.append(pltpu.make_async_copy(text_ref.at[:, pl.ds(column, width)], text, sems.at[4]))
    for copy in copies:
        copy.start()
    for at, (hop, out) in enumerate(zip(HOPS, outs)):
        copies[at].wait()
        total = jnp.dot(attended_ref[...], weights[at], preferred_element_type=jnp.float32)
        if hop == 0:
            copies[4].wait()
            total = text[...].astype(jnp.float32) + gate_ref[...] * total
        out[...] = total


def project_own(me, gate, attended, w_out, text):
    rows, width = attended.shape[0], w_out.shape[1] // 8
    return pl.pallas_call(
        own_kernel,
        out_shape=[jax.ShapeDtypeStruct((rows, width), jnp.float32)] * 4,
        in_specs=[SMEM, VMEM, VMEM, HBM, HBM],
        out_specs=[VMEM] * 4,
        scratch_shapes=[
            pltpu.VMEM((4, w_out.shape[0], width), jnp.bfloat16),
            pltpu.VMEM((rows, width), jnp.bfloat16),
            pltpu.SemaphoreType.DMA((5,)),
        ],
        compiler_params=params(46),
        cost_estimate=HINT,
        name="project_own",
    )(me, gate, attended, w_out, text)


def out_kernel(jobs, me_ref, gate_ref, swapped_ref, *refs):
    own, mine, other, outs = refs[:4], refs[4:8], refs[8:12], refs[12:]
    y, core, z = me_ref[0] >> 2, me_ref[0] & 1, me_ref[1] >> 1
    rows = mine[0].shape[0]
    tile = mine[0].shape[1] // 4
    swapped = jnp.concatenate(
        [swapped_ref[:, pl.ds(pl.multiple_of(((y - back) & 3) * rows, rows), rows)] for back in [0] + RING], axis=1
    )
    for (hops, start, stop), out in zip(jobs, outs):
        for at, hop in enumerate(hops):
            source = pl.ds(pl.multiple_of((z ^ hop) * tile, tile), tile)
            band = slice(at * (stop - start), (at + 1) * (stop - start))
            for half, pieces in ((core, mine), (1 - core, other)):
                target = pl.ds(pl.multiple_of(half * tile, tile), tile)
                weight = jnp.concatenate([piece[:, source] for piece in pieces], axis=0)
                product = jnp.dot(swapped[start:stop], weight, preferred_element_type=jnp.float32)
                if hop == 0:
                    product = gate_ref[...] * product
                total = own[HOPS.index(hop)][start:stop, target] + product
                out[band, target] = total.astype(out.dtype)


def project_out(jobs, dtype, me, gate, swapped, own, mine, other):
    width = own[0].shape[1]
    return pl.pallas_call(
        functools.partial(out_kernel, jobs),
        out_shape=[jax.ShapeDtypeStruct((len(hops) * (stop - start), width), dtype) for hops, start, stop in jobs],
        in_specs=[SMEM] + [VMEM] * 14,
        out_specs=[VMEM] * len(jobs),
        compiler_params=params(32),
        cost_estimate=HINT,
        name="project_out",
    )(me, gate, swapped, *own, *mine, *other)


def relay_kernel(kept_ref, arrived_ref, out_ref):
    rows = out_ref.shape[0]
    out_ref[...] = (kept_ref[...] + arrived_ref[rows:].astype(jnp.float32)).astype(out_ref.dtype)


def relay(kept, arrived):
    return pl.pallas_call(
        relay_kernel,
        out_shape=jax.ShapeDtypeStruct(kept.shape, jnp.bfloat16),
        in_specs=[VMEM] * 2,
        out_specs=VMEM,
        compiler_params=params(16),
        cost_estimate=HINT,
        name="relay",
    )(kept, arrived)


def add_kernel(base_ref, gate_ref, *refs):
    arrived, out_ref = refs[:-1], refs[-1]
    rows = out_ref.shape[0] // 2
    for at in range(2):
        band = slice(at * rows, (at + 1) * rows)
        total = arrived[at][:rows].astype(jnp.float32) + arrived[2 + at][...].astype(jnp.float32)
        out_ref[band] = (base_ref[band] + gate_ref[...] * total).astype(jnp.bfloat16)


def local(
    text_states,
    image_states,
    counts,
    norm_gain,
    w_query,
    q_gain,
    w_key,
    w_value,
    k_gain,
    w_out,
    attn_gate,
):
    tp_me = lax.axis_index("tp")
    ctx_me = lax.axis_index("ctx")
    ctx_row = ctx_me.astype(jnp.int32).reshape(1)
    me = jnp.stack([ctx_me, tp_me]).astype(jnp.int32)

    cut = cut_weights(ctx_me, tp_me, w_out)
    image_states, text_first, cut = lax.optimization_barrier((image_states, text_states, cut))
    piece = tp_send(cut, (0, 1))
    sent = project_kv(image_states.T, w_key, w_value)
    sent, piece = lax.optimization_barrier((sent, piece))
    mine = [piece] + [ctx_send(piece, (ring, 0, 0)) for ring in RING]
    arrived = lax.all_to_all(sent, "tp", 0, 0, tiled=True)
    query = project_query(text_first, norm_gain, w_query, q_gain)
    arrived, query = lax.optimization_barrier((arrived, query))
    own_kv = combine_kv(k_gain, arrived)

    far = [ctx_send(own_kv, shift + (0,)) for shift in AROUND[:-1]] + [own_kv]
    near = [ctx_send(block, (0, 0, 1)) for block in far]
    far[0], *mine = lax.optimization_barrier((far[0], *mine))
    held = attend(ctx_row, counts, query, far, 0)
    (attended,) = attend(ctx_row, counts, query, near, 1, held)
    other = [ctx_send(block, (0, 0, 1)) for block in mine]

    gate = jnp.tanh(attn_gate).reshape(1, 1)
    swapped = tp_send(attended, (0, 1))
    own = project_own(me, gate, attended, w_out, text_states)
    rows = text_states.shape[0]
    low, high = (0, rows // 2), (rows // 2, rows)
    operands = (me, gate, swapped, own, mine, other)
    (first_low,) = project_out([((1, 2), *low)], jnp.bfloat16, *operands)
    low_arrived = hop_send(first_low, 1)
    (first_high,) = project_out([((3, 2), *high)], jnp.bfloat16, *operands)
    high_arrived = hop_send(first_high, 3)
    kept_low, kept_high, base = project_out([((3,), *low), ((1,), *high), ((0,), 0, rows)], jnp.float32, *operands)
    low_last = hop_send(relay(kept_low, low_arrived), 3)
    high_last = hop_send(relay(kept_high, high_arrived), 1)
    arrived = [low_arrived, high_arrived, low_last, high_last]
    return pl.pallas_call(
        add_kernel,
        out_shape=jax.ShapeDtypeStruct(base.shape, jnp.bfloat16),
        in_specs=[VMEM] * (2 + len(arrived)),
        out_specs=VMEM,
        compiler_params=params(16),
        cost_estimate=HINT,
        name="add_residual",
    )(base, gate, *arrived)


def solution(mesh):
    in_specs = (
        P("ctx", None),
        P("ctx", "tp"),
        P(),
        P(),
        P(None, "tp"),
        P(),
        P("tp", None),
        P("tp", None),
        P(),
        P("tp", None),
        P(),
    )
    out_specs = P("ctx", "tp")
    return jax.shard_map(local, mesh=mesh, in_specs=in_specs, out_specs=out_specs, check_vma=False)
```
